512 devices in a mesh: tile: 128 (over y, z, core), lev: 4 (over x).
Axes of the slice: x: 4, y: 8, z: 8, core: 2. Of those that a mesh axis runs over, the one named last changes fastest.
Arguments:
- field: float32 [8, 256, 4096], P('lev', 'tile'), may hold values from -6 to 6
- kappa_sq: float32 [8, 256, 4096], P('lev', 'tile'), may hold values from 0.25 to 4
- noise: float32 [3, 8, 256, 4096], P(None, 'lev', 'tile'), may hold values from -6 to 6
- block_owner: int32 [8, 8192, 1], P('lev', 'tile'), may hold values from 0 to 127; in each aligned block of 64 rows (0 to 63, 64 to 127, ..., all dimensions but the last counted through in order) at most 2 rows name the same one
- block_cell: int32 [8, 8192], P('lev', 'tile'), may hold values from 0 to 63
- live_count: int32 [8, 128], P('lev', 'tile'), may hold values from 16 to 64, as said below
- obs_weight: bfloat16 [8, 8192, 16, 128], P('lev', 'tile'), may hold values from -0.5 to 0.5
- obs_value: float32 [8, 8192, 16], P('lev', 'tile'), may hold values from -6 to 6
- obs_prec: float32 [8, 8192, 16], P('lev', 'tile'), may hold values from 1 to 32
Outputs:
- sample: float32 [8, 256, 4096], P('lev', 'tile')
The draws below stay inside these ranges and needn't reach their ends.
Inputs may be any that keep to these rules, and one draw needn't show every extreme that they name: `block_owner`: among the blocks of one shard (aligned blocks of 64) and one level, at most 2 name the same owner tile. `live_count`: some shard has all its blocks of level 0 live.
All inputs are finite; a program needn't handle non-finite values.
Results may differ from the reference program's by a relative error of at most 0.00085.
Values may be sent and summed in bfloat16 or wider, within the bound.
A program may use at most 64 MiB of HBM per device.

```python
import math
import jax
import jax.numpy as jnp
import numpy as np
from jax import lax

NX = 4096
BLKC = 128
OBS_BLK = 16
BLK_DEV = 64
STEPS = 3
CAP = 2
SEG_DEV = 64
LEVELS = 8
NY = 256
BLKS = 8192
N_TILE = 128


def draw_live_count(key, part):
    key = jax.random.fold_in(key, 5)
    first_key, second_key = jax.random.split(key)
    shard_total = BLKS // BLK_DEV
    counts = jax.random.randint(first_key, (LEVELS, shard_total), BLK_DEV // 4, BLK_DEV + 1, dtype=jnp.int32)
    chosen = jax.random.randint(second_key, (), 0, shard_total, dtype=jnp.int32)
    return counts.at[0, chosen].set(BLK_DEV).astype(jnp.int32)


def set_ends(values, stream_key, smallest, high):
    place = [jax.random.randint(jax.random.fold_in(stream_key, axis), (), 0, length) for axis, length in enumerate(values.shape)]
    longest = values.shape.index(max(values.shape))
    beside = place[:longest] + [(place[longest] + 1) % values.shape[longest]] + place[longest + 1:]
    return values.at[tuple(place)].set(smallest).at[tuple(beside)].set(high)


def level_of(stream_key, shape, cuts, low, top_value):
    def one(dim, parts):
        draws = jax.random.uniform(jax.random.fold_in(jax.random.fold_in(stream_key, 6), dim), (parts,), jnp.float32, low / len(cuts), top_value / len(cuts))
        return jnp.repeat(jnp.exp(draws), shape[dim] // parts).reshape((-1,) + (1,) * (len(shape) - dim - 1))

    factor_of = one(*cuts[0])
    for cut in cuts[1:]:
        factor_of = factor_of * one(*cut)
    return factor_of


def assign_block(stream_key, own, number, rows, number_of, top, bound, slope):
    sequence = jax.random.permutation(stream_key, number_of)
    crowded, ordinary = portions_of(number_of, rows * top, bound, slope, True), portions_of(number_of, rows * top, bound, slope, False)
    places = jnp.arange(number_of)

    def named(tallies, offset_by):
        used = int((tallies > 0).sum())
        fixed = max(1, used // 4)
        moved = fixed + (places - fixed + offset_by * (used - fixed)) % max(1, number_of - fixed)
        return jnp.zeros((number_of,), jnp.int32).at[sequence[jnp.where(places < fixed, places, moved)]].set(jnp.asarray(tallies, jnp.int32))

    tallies = jnp.where(number % 4 == 0, named(crowded, number // 4), named(ordinary, number - number // 4 - 1))
    mixed = jax.random.permutation(jax.random.fold_in(own, 3), number_of)
    source_of, taker = mixed[0:number_of // 2 * 2:2], mixed[1:number_of // 2 * 2:2]
    room = jnp.minimum(tallies[source_of] - 1, bound - tallies[taker]) // 2
    room = jnp.where((source_of == sequence[0]) | (taker == sequence[0]) | (tallies[taker] == 0), 0, jnp.maximum(room, 0))
    moved = jax.random.randint(jax.random.fold_in(own, 4), (number_of // 2,), 0, 1 << 20) % (room + 1)
    tallies = tallies.at[source_of].add(-moved).at[taker].add(moved)
    labels = jnp.searchsorted(jnp.cumsum(tallies), jnp.arange(rows * top), side="right").astype(jnp.int32)
    grid = labels.reshape(top, rows).T
    grid = grid[jax.random.permutation(jax.random.fold_in(own, 1), rows)]
    offset_by = jax.random.randint(jax.random.fold_in(own, 2), (rows, 1), 0, top)
    return jnp.take_along_axis(grid, (jnp.arange(top)[None, :] + offset_by) % top, axis=1)


def portions_of(number_of, total, reach, skew, full):
    loads = [(1 << 20) // math.isqrt(grade ** skew) + 1 for grade in range(1, number_of + 1)]
    largest = reach if full else min(reach, max(-(-total // number_of), total * loads[0] // sum(loads)))
    least = 1 if total - largest >= number_of - 1 else 0
    given, spare = [largest] + [least] * (number_of - 1), total - largest - least * (number_of - 1)
    while spare > 0:
        candidates = [i for i in range(1, number_of) if given[i] < largest] or [i for i in range(1, number_of) if given[i] < reach]
        whole, remaining = sum([loads[i] for i in candidates]), spare
        for i in candidates:
            extra = min(reach - given[i], max(1, remaining * loads[i] // whole), spare)
            given[i] = given[i] + extra
            spare = spare - extra
    return np.array(given)


def centred(rng, extent, scale, reach, shards=(), kind=jnp.bfloat16):
    entries = jax.random.normal(rng, extent, jnp.float32) * scale
    if len(shards) > 0:
        entries = level_of(rng, extent, shards, -0.22, 0.18) * entries
    return jnp.clip(entries, min=-reach, max=reach).astype(kind)


def setup_inputs(seed: int = 0) -> dict:
    arg_keys = jax.random.split(jax.random.key(seed), 10)
    field = centred(arg_keys[0], (LEVELS, NY, NX), 1.0, 6.0, ((0, 4), (1, 128)), jnp.float32)
    kappa_sq = jnp.clip(jnp.exp(math.log(4.0) - 2.7725887 * jax.random.uniform(arg_keys[1], (LEVELS, NY, NX), jnp.float32) ** level_of(arg_keys[1], (LEVELS, NY, NX), ((0, 4), (1, 128)), -0.2, 0.2)), 0.25, 4.0)
    noise = centred(arg_keys[2], (STEPS, LEVELS, NY, NX), 1.0, 6.0, ((1, 4), (2, 128)), jnp.float32)
    block_owner_keys = jax.random.split(jax.random.fold_in(arg_keys[3], 1), LEVELS * BLKS // BLK_DEV)
    block_owner_turns = jax.random.permutation(jax.random.fold_in(arg_keys[3], 3), LEVELS * BLKS // BLK_DEV)
    block_owner = jax.vmap(lambda own, number: assign_block(jax.random.fold_in(arg_keys[3], 2), own, number, BLK_DEV, N_TILE, 1, CAP, 2))(block_owner_keys, block_owner_turns).reshape((LEVELS, BLKS, 1))
    block_cell = set_ends(jax.random.randint(arg_keys[4], (LEVELS, BLKS), 0, SEG_DEV), jax.random.fold_in(arg_keys[4], 1), 0, SEG_DEV - 1).astype(jnp.int32)
    live_count = draw_live_count(jax.random.fold_in(arg_keys[9], 71), 0)
    obs_weight = centred(arg_keys[6], (LEVELS, BLKS, OBS_BLK, BLKC), BLKC ** -0.5, 0.5, ((0, 4), (1, 128)))
    obs_value = centred(arg_keys[7], (LEVELS, BLKS, OBS_BLK), 1.0, 6.0, ((0, 4), (1, 128)), jnp.float32)
    obs_prec = jnp.clip(jnp.exp(math.log(32.0) - 3.465736 * jax.random.uniform(arg_keys[8], (LEVELS, BLKS, OBS_BLK), jnp.float32) ** level_of(arg_keys[8], (LEVELS, BLKS, OBS_BLK), ((0, 4), (1, 128)), -0.2, 0.2)), 1.0, 32.0)
    return {"field": field, "kappa_sq": kappa_sq, "noise": noise, "block_owner": block_owner, "block_cell": block_cell, "live_count": live_count, "obs_weight": obs_weight, "obs_value": obs_value, "obs_prec": obs_prec}


step_size = 0.003

def stencil(padded, kappa_in):
    core = padded[1:-1, 1:-1]
    near = padded[:-2, 1:-1] + padded[2:, 1:-1] + padded[1:-1, :-2] + padded[1:-1, 2:]
    near = near + jnp.roll(core, 1, 2) + jnp.roll(core, -1, 2)
    return (kappa_in + 6.0) * core - near

def operate(values, kappa_sq):
    return stencil(jnp.pad(values, ((1, 1), (1, 1), (0, 0))), kappa_sq)

def reference(field, kappa_sq, noise, block_owner, block_cell, live_count, obs_weight, obs_value, obs_prec):
    owners = block_owner[:, :, 0]
    block_ids = jnp.arange(BLKS, dtype=jnp.int32)
    counts = live_count[:, block_ids // BLK_DEV]
    alive = ((block_ids % BLK_DEV)[None, :] < counts).astype(jnp.float32)
    noise_scale = (2.0 * step_size) ** 0.5

    def level_grad(inputs):
        segments, owner_row, cell_row, weights, observed, precision, alive_row = inputs
        gathered = segments[owner_row, cell_row]
        weight_f = weights.astype(jnp.float32)
        predicted = jnp.einsum('boc,bc->bo', weight_f, gathered, precision=lax.Precision.HIGHEST)
        misfit = precision * alive_row[:, None] * (predicted - observed)
        adjoint = jnp.einsum('boc,bo->bc', weight_f, misfit, precision=lax.Precision.HIGHEST)
        return jnp.zeros_like(segments).at[owner_row, cell_row].add(adjoint)
    state = field
    for step_index in range(STEPS):
        segments = state.reshape(LEVELS, N_TILE, SEG_DEV, BLKC)
        obs_grad = lax.map(level_grad, (segments, owners, block_cell, obs_weight, obs_value, obs_prec, alive))
        obs_grad = obs_grad.reshape(LEVELS, NY, NX)
        prior = operate(operate(state, kappa_sq), kappa_sq)
        state = state - step_size * (prior + obs_grad) + noise_scale * noise[step_index]
    return state
```

```python
import jax
import jax.numpy as jnp
from jax import lax
from jax.sharding import PartitionSpec as P
from jax.experimental import pallas as pl
from jax.experimental.pallas import tpu as pltpu

STEPS = 3
STEP = 0.003
NOISE_SCALE = (2.0 * STEP) ** 0.5
MESH = pl.DeviceIdType.MESH
BF = jnp.bfloat16
F32 = jnp.float32
RING = 8


def ring_distance(d):
    return min(d, RING - d)


def hops(delta):
    return ring_distance(delta[0]) + ring_distance(delta[1])


PEERS = sorted(
    [(a, b, c) for a in range(RING) for b in range(RING) for c in range(2) if (a, b, c) != (0, 0, 0)],
    key=lambda d: (-hops(d), (d[0] + 3 * d[1]) % 4, d),
)
SELF = len(PEERS)
GROUPS = SELF + 1
SLOTS = 4
ROWS = GROUPS * SLOTS


def dot(a, b, dims=((1,), (0,)), **kw):
    return lax.dot_general(a, b, (dims, ((), ())), preferred_element_type=F32, **kw)


def iota(shape, dim):
    return lax.broadcasted_iota(jnp.int32, shape, dim)


def kernel_body(
    slot_ref, field_ref, kappa_ref, noise_ref, owner_ref, cell_ref, live_ref, weight_ref, value_ref, prec_ref,
    out_ref,
    trip_out, trip_in, halo_x, halo_k, x_buf, k_buf, pick_ref, pick_t_ref, gain_ref, offset_ref, weight_t_ref,
    trip_send, trip_recv, halo_send, halo_recv,
):
    me = lax.axis_index("tile")
    lev = lax.axis_index("lev")
    tiles = 2 * RING * RING
    y, z, c = me // (2 * RING), (me // 2) % RING, me % 2
    at_y = [((y + d) % RING) * (2 * RING) for d in range(RING)]
    at_z = [((z + d) % RING) * 2 for d in range(RING)]
    at_c = [c, 1 - c]

    def peer(delta):
        return at_y[delta[0]] + at_z[delta[1]] + at_c[delta[2]]

    above, below = (lev + 1) % 4, (lev + 3) % 4
    north, south = (me + 1) % tiles, (me + tiles - 1) % tiles

    greet = pltpu.get_barrier_semaphore()
    for delta in PEERS:
        pl.semaphore_signal(greet, inc=1, device_id=(peer(delta), lev), device_id_type=MESH)
    beside = [(me, above), (me, below), (north, above), (north, below), (south, above), (south, below)]
    for device in beside:
        pl.semaphore_signal(greet, inc=1, device_id=device, device_id_type=MESH)

    for l in range(2):
        for r in range(2):
            x_buf[0, 2 * l + r] = field_ref[l, r : r + 1, :].reshape(32, 128)
            k_buf[2 * l + r] = kappa_ref[l, r : r + 1, :].reshape(32, 128)

    owner = owner_ref[...].reshape(128, 1)
    level_of = iota((128, 1), 0) // 64
    slot_peer = slot_ref[0:1, :]
    slot_y, slot_z, slot_c = slot_ref[1:2, :], slot_ref[2:3, :], slot_ref[3:4, :]
    slot_peer = ((y + slot_y) % RING) * (2 * RING) + ((z + slot_z) % RING) * 2 + (c + slot_c) % 2
    slot_j = iota((1, ROWS), 1) % SLOTS
    row_i, col_i = iota((128, 128), 0), iota((128, 128), 1)
    named = (owner == col_i).astype(F32)
    before = ((col_i < row_i) & (col_i // 64 == row_i // 64)).astype(BF)
    rank = jnp.sum(dot(before, named.astype(BF)) * named, axis=1, keepdims=True)
    block_j = 2 * level_of + rank.astype(jnp.int32)
    pick = ((owner == slot_peer) & (block_j == slot_j)).astype(F32)
    pick_ref[...] = pick.astype(BF)
    pick_t = pick.T.astype(BF)
    pick_t_ref[...] = pick_t
    cells = jnp.concatenate([cell_ref[0:1, :], cell_ref[1:2, :]], axis=1)
    cell_t = ((row_i // 64 == col_i // 64) & (row_i % 64 == cells)).astype(BF)
    request = dot(pick_t, cell_t, ((1,), (1,))).astype(BF).reshape(GROUPS, SLOTS, 128)
    trip_out[0] = request
    trip_in[0, SELF] = request[SELF]

    alive = jnp.concatenate(
        [(iota((64, 1), 0) < live_ref[l : l + 1, :]).astype(F32) for l in range(2)], axis=0
    )
    spread = (iota((16, 256), 1) % 16 == iota((16, 256), 0)).astype(F32)
    own = (iota((128, 256), 1) // 16 == iota((128, 256), 0) % 16).astype(F32)
    gain = prec_ref[...].reshape(128, 16) * alive
    offset = gain * value_ref[...].reshape(128, 16)
    gain_ref[...] = dot(gain, spread, precision=lax.Precision.HIGHEST) * own
    offset_ref[...] = dot(offset, spread, precision=lax.Precision.HIGHEST) * own
    for p in range(8):
        w = weight_ref[p // 4, 16 * (p % 4) : 16 * (p % 4) + 16].reshape(256, 128)
        weight_t_ref[p] = w.T

    pl.semaphore_wait(greet, len(PEERS) + len(beside))

    def trip_copy(t, i, delta):
        if t % 2:
            delta = ((RING - delta[0]) % RING, (RING - delta[1]) % RING, delta[2])
        return pltpu.make_async_remote_copy(
            trip_out.at[t, i], trip_in.at[t, i], trip_send.at[t], trip_recv.at[t],
            device_id=(peer(delta), lev), device_id_type=MESH,
        )

    def trip_all(t):
        return pltpu.make_async_remote_copy(
            trip_out.at[t, pl.ds(0, SELF)], trip_in.at[t, pl.ds(0, SELF)], trip_send.at[t], trip_recv.at[t],
            device_id=(north, lev), device_id_type=MESH,
        )

    def start_trip(t):
        for i, delta in enumerate(PEERS):
            trip_copy(t, i, delta).start()

    def halo_copy(src, dst, s, device):
        return pltpu.make_async_remote_copy(
            src, dst, halo_send.at[s], halo_recv.at[s], device_id=device, device_id_type=MESH
        )

    def start_halo(k):
        x = x_buf.at[k]
        into = halo_x.at[k]
        halo_copy(x, into.at[pl.ds(0, 4)], k, (me, above)).start()
        halo_copy(x, into.at[pl.ds(4, 4)], k, (me, below)).start()
        halo_copy(x, into.at[pl.ds(8, 4)], k, (north, lev)).start()
        halo_copy(x, into.at[pl.ds(12, 4)], k, (south, lev)).start()
        halo_copy(x.at[3], into.at[16], k, (north, above)).start()
        halo_copy(x.at[2], into.at[17], k, (south, above)).start()
        halo_copy(x.at[1], into.at[18], k, (north, below)).start()
        halo_copy(x.at[0], into.at[19], k, (south, below)).start()

    def halo_all(k):
        return halo_copy(halo_x.at[k], halo_x.at[k], k, (north, lev))

    def start_kappa():
        halo_copy(k_buf.at[pl.ds(2, 2)], halo_k.at[pl.ds(0, 2)], STEPS, (me, above)).start()
        halo_copy(k_buf.at[pl.ds(0, 2)], halo_k.at[pl.ds(2, 2)], STEPS, (me, below)).start()
        for l in range(2):
            halo_copy(k_buf.at[2 * l + 1], halo_k.at[4 + l], STEPS, (north, lev)).start()
            halo_copy(k_buf.at[2 * l], halo_k.at[6 + l], STEPS, (south, lev)).start()

    def kappa_all():
        return halo_copy(halo_k, halo_k, STEPS, (north, lev))

    start_trip(0)
    start_halo(0)
    start_kappa()

    lane = iota((32, 128), 1)
    has = {
        (-1, 0): lev > 0, (1, 0): lev < 3, (0, -1): me > 0, (0, 1): me < tiles - 1,
    }

    def stencil(v, kap, near):
        left = pltpu.roll(v, 1, 1)
        left = jnp.where(lane == 0, pltpu.roll(left, 1, 0), left)
        right = pltpu.roll(v, 127, 1)
        right = jnp.where(lane == 127, pltpu.roll(right, 31, 0), right)
        return (kap + 6.0) * v - (near + left + right)

    def prior(k):
        halo_all(k).wait_recv()
        if k == 0:
            kappa_all().wait_recv()
        v, kap = {}, {}
        for l in range(2):
            for r in range(2):
                v[l, r] = x_buf[k, 2 * l + r]
                kap[l, r] = k_buf[2 * l + r]
                v[l - 2, r] = halo_x[k, 2 * l + r]
                v[l + 2, r] = halo_x[k, 4 + 2 * l + r]
                v[l, r - 2] = halo_x[k, 8 + 2 * l + r]
                v[l, r + 2] = halo_x[k, 12 + 2 * l + r]
        v[-1, -1], v[-1, 2], v[2, -1], v[2, 2] = (halo_x[k, 16 + q] for q in range(4))
        for q in range(2):
            kap[-1, q], kap[2, q] = halo_k[q], halo_k[2 + q]
            kap[q, -1], kap[q, 2] = halo_k[4 + q], halo_k[6 + q]

        def inside(l, r):
            conds = []
            if l < 0:
                conds.append(has[-1, 0])
            if l > 1:
                conds.append(has[1, 0])
            if r < 0:
                conds.append(has[0, -1])
            if r > 1:
                conds.append(has[0, 1])
            return conds

        def masked(p, l, r):
            for cond in inside(l, r):
                p = jnp.where(cond, p, 0.0)
            return p

        v = {at: masked(p, *at) for at, p in v.items()}
        once = {}
        for l, r in list(kap):
            near = v[l - 1, r] + v[l + 1, r] + v[l, r - 1] + v[l, r + 1]
            once[l, r] = masked(stencil(v[l, r], kap[l, r], near), l, r)
        planes = []
        for l in range(2):
            for r in range(2):
                near = once[l - 1, r] + once[l + 1, r] + once[l, r - 1] + once[l, r + 1]
                twice = stencil(once[l, r], kap[l, r], near)
                noise = noise_ref[k, l, r : r + 1, :].reshape(32, 128)
                planes.append(v[l, r] - STEP * twice + NOISE_SCALE * noise)
        return planes

    wanted = None
    for k in range(STEPS):
        x = x_buf[k].reshape(128, 128).astype(BF)
        if k == 0:
            trip_all(0).wait_recv()
            wanted = trip_in[0].reshape(ROWS, 128)
        send = dot(wanted, x).astype(BF).reshape(GROUPS, SLOTS, 128)
        trip_out[1 + 2 * k] = send
        trip_in[1 + 2 * k, SELF] = send[SELF]
        start_trip(1 + 2 * k)
        if k > 0:
            start_halo(k)
        planes = prior(k)
        trip_all(1 + 2 * k).wait_recv()
        cells_in = dot(pick_ref[...], trip_in[1 + 2 * k].reshape(ROWS, 128)).astype(BF)
        parts = []
        for p in range(8):
            seen = dot(cells_in[16 * p : 16 * p + 16], weight_t_ref[p])
            misfit = gain_ref[16 * p : 16 * p + 16] * seen - offset_ref[16 * p : 16 * p + 16]
            w = weight_ref[p // 4, 16 * (p % 4) : 16 * (p % 4) + 16].reshape(256, 128)
            parts.append(dot(misfit.astype(BF), w).astype(BF))
        adjoint = jnp.concatenate(parts, axis=0)
        send = dot(pick_t_ref[...], adjoint).astype(BF).reshape(GROUPS, SLOTS, 128)
        trip_out[2 + 2 * k] = send
        trip_in[2 + 2 * k, SELF] = send[SELF]
        start_trip(2 + 2 * k)
        trip_all(2 + 2 * k).wait_recv()
        total = dot(wanted, trip_in[2 + 2 * k].reshape(ROWS, 128), ((0,), (0,)))
        for l in range(2):
            for r in range(2):
                q = 2 * l + r
                new = planes[q] - STEP * total[32 * q : 32 * q + 32]
                if k + 1 < STEPS:
                    x_buf[k + 1, q] = new
                else:
                    out_ref[l, r : r + 1, :] = new.reshape(1, 4096)

    for t in range(1 + 2 * STEPS):
        trip_all(t).wait_send()
    for k in range(STEPS):
        halo_all(k).wait_send()
    kappa_all().wait_send()


def per_device(slots, *arrays):
    vmem = pl.BlockSpec(memory_space=pltpu.VMEM)
    trips = 1 + 2 * STEPS
    return pl.pallas_call(
        kernel_body,
        out_shape=jax.ShapeDtypeStruct((2, 2, 4096), F32),
        in_specs=[vmem] * 10,
        out_specs=vmem,
        scratch_shapes=[
            pltpu.VMEM((trips, GROUPS, SLOTS, 128), BF),
            pltpu.VMEM((trips, GROUPS, SLOTS, 128), BF),
            pltpu.VMEM((STEPS, 20, 32, 128), F32),
            pltpu.VMEM((8, 32, 128), F32),
            pltpu.VMEM((STEPS, 4, 32, 128), F32),
            pltpu.VMEM((4, 32, 128), F32),
            pltpu.VMEM((128, ROWS), BF),
            pltpu.VMEM((ROWS, 128), BF),
            pltpu.VMEM((128, 256), F32),
            pltpu.VMEM((128, 256), F32),
            pltpu.VMEM((8, 128, 256), BF),
            pltpu.SemaphoreType.DMA((trips,)),
            pltpu.SemaphoreType.DMA((trips,)),
            pltpu.SemaphoreType.DMA((STEPS + 1,)),
            pltpu.SemaphoreType.DMA((STEPS + 1,)),
        ],
        compiler_params=pltpu.CompilerParams(
            collective_id=0, has_side_effects=True, vmem_limit_bytes=48 << 20
        ),
        cost_estimate=pl.CostEstimate(flops=200_000_000, bytes_accessed=1_000_000, transcendentals=0),
    )(slots, *arrays)


def slot_table():
    deltas = PEERS + [(0, 0, 0)]
    table = [[0] * ROWS for _ in range(8)]
    for i, delta in enumerate(deltas):
        for j in range(SLOTS):
            for q in range(3):
                table[1 + q][SLOTS * i + j] = delta[q]
    return jnp.array(table, jnp.int32)


def solution(mesh):
    placed = (
        P("lev", "tile", None),
        P("lev", "tile", None),
        P(None, "lev", "tile", None),
        P("lev", "tile", None),
        P("lev", "tile"),
        P("lev", "tile"),
        P("lev", "tile", None, None),
        P("lev", "tile", None),
        P("lev", "tile", None),
    )
    run = jax.shard_map(
        per_device, mesh=mesh, in_specs=(P(None, None),) + placed, out_specs=P("lev", "tile", None), check_vma=False
    )

    def sample(*arrays):
        return run(slot_table(), *arrays)

    return sample
```

```python
import jax
import jax.numpy as jnp
from jax import lax
from jax.sharding import PartitionSpec as P
from jax.experimental import pallas as pl
from jax.experimental.pallas import tpu as pltpu

STEPS = 3
STEP = 0.003
NOISE_SCALE = (2.0 * STEP) ** 0.5
MESH = pl.DeviceIdType.MESH
BF = jnp.bfloat16
F32 = jnp.float32
RING = 8


def ring_distance(d):
    return min(d, RING - d)


def hops(delta):
    return ring_distance(delta[0]) + ring_distance(delta[1])


PEERS = sorted(
    [(a, b, c) for a in range(RING) for b in range(RING) for c in range(2) if (a, b, c) != (0, 0, 0)],
    key=lambda d: (-hops(d), (d[0] + 3 * d[1]) % 4, d),
)
SELF = len(PEERS)
GROUPS = SELF + 1
SLOTS = 4
ROWS = GROUPS * SLOTS
FAR = 32

OUTWARD = (4, 3, 5, 2, 6, 1, 7)
LINE_ROWS = 2 * RING


def along(l, e):
    return (e, 0, 0) if l == 0 else (0, e, 0)


def across(l, q):
    return (0, q // 2, q % 2) if l == 0 else (q // 2, 0, q % 2)


def negative(delta):
    return ((RING - delta[0]) % RING, (RING - delta[1]) % RING, delta[2])


ACROSS = [2 * d + c for d in OUTWARD for c in (1, 0)] + [1]
GREETED = sorted({across(l, q) for l in range(2) for q in ACROSS})


def dot(a, b, dims=((1,), (0,)), **kw):
    return lax.dot_general(a, b, (dims, ((), ())), preferred_element_type=F32, **kw)


def iota(shape, dim):
    return lax.broadcasted_iota(jnp.int32, shape, dim)


def kernel_body(
    slot_hbm, field_hbm, kappa_hbm, noise_hbm, owner_hbm, cell_hbm, live_hbm, weight_hbm, value_hbm, prec_hbm,
    out_ref,
    slot_ref, field_ref, kappa_ref, noise_ref, owner_ref, cell_ref, live_ref, weight_ref, value_ref, prec_ref,
    trip_out, trip_in, halo_x, halo_k, x_buf, k_buf, pick_ref, pick_t_ref, gain_ref, offset_ref, weight_t_ref,
    wanted_t_ref, seed_out, seed_in, ask_out, ask_in, answer_out, answer_in, pick_line_ref,
    trip_send, trip_recv, halo_send, halo_recv, load_sem, line_send, line_recv,
):
    me = lax.axis_index("tile")
    lev = lax.axis_index("lev")
    tiles = 2 * RING * RING
    y, z, c = me // (2 * RING), (me // 2) % RING, me % 2
    at_y = [((y + d) % RING) * (2 * RING) for d in range(RING)]
    at_z = [((z + d) % RING) * 2 for d in range(RING)]
    at_c = [c, 1 - c]

    def peer(delta):
        return at_y[delta[0]] + at_z[delta[1]] + at_c[delta[2]]

    above, below = (lev + 1) % 4, (lev + 3) % 4
    north, south = (me + 1) % tiles, (me + tiles - 1) % tiles

    greet = pltpu.get_barrier_semaphore()
    for delta in GREETED:
        pl.semaphore_signal(greet, inc=1, device_id=(peer(delta), lev), device_id_type=MESH)
    beside = [(north, lev), (south, lev), (me, above), (me, below), (north, above), (north, below), (south, above), (south, below)]
    for device in beside:
        pl.semaphore_signal(greet, inc=1, device_id=device, device_id_type=MESH)

    loads = [
        pltpu.make_async_copy(src, dst, load_sem.at[i])
        for i, (src, dst) in enumerate(
            [
                (owner_hbm, owner_ref), (cell_hbm, cell_ref), (slot_hbm, slot_ref), (field_hbm, field_ref),
                (kappa_hbm, kappa_ref), (live_hbm, live_ref), (prec_hbm, prec_ref), (value_hbm, value_ref),
                (weight_hbm, weight_ref), (noise_hbm, noise_ref),
            ]
        )
    ]
    for load in loads:
        load.start()
    for load in loads[:5]:
        load.wait()
    for l in range(2):
        for r in range(2):
            x_buf[0, 2 * l + r] = field_ref[l, r : r + 1, :].reshape(32, 128)
            k_buf[2 * l + r] = kappa_ref[l, r : r + 1, :].reshape(32, 128)

    owner_row = jnp.concatenate([owner_ref[0], owner_ref[1]], axis=1).astype(F32)
    owner = jnp.broadcast_to(owner_row, (128, 128)).T.astype(jnp.int32)[:, 0:1]
    level_of = iota((128, 1), 0) // 64
    row_i, col_i = iota((128, 128), 0), iota((128, 128), 1)
    named = (owner == col_i).astype(F32)
    before = ((col_i < row_i) & (col_i // 64 == row_i // 64)).astype(BF)
    rank = jnp.sum(dot(before, named.astype(BF)) * named, axis=1, keepdims=True).astype(jnp.int32)
    n = iota((1, 256), 1)
    for l in range(2):
        x_flat = jnp.concatenate([x_buf[0, 2 * l], x_buf[0, 2 * l + 1]], axis=0).astype(BF)
        seed_out[l] = x_flat
        seed_in[l, 0] = x_flat
        e, d = (n // 2) % RING, n // 32
        dy, dz = (e, d) if l == 0 else (d, e)
        line_peer = ((y + dy) % RING) * (2 * RING) + ((z + dz) % RING) * 2 + (c + (n // 16) % 2) % 2
        mine = slice(64 * l, 64 * l + 64)
        pick_line = ((owner[mine] == line_peer) & (rank[mine] == n % 2)).astype(F32)
        pick_line_ref[l] = pick_line.astype(BF)
        cell_line = (row_i[:, :64] % 64 == cell_ref[l : l + 1, :]).astype(F32).T.astype(BF)
        ask = dot(pick_line.T.astype(BF), cell_line).astype(BF).reshape(2 * RING, LINE_ROWS, 128)
        ask_out[l] = ask
        ask_in[l, 0] = ask[0]

    pl.semaphore_wait(greet, len(GREETED) + len(beside))

    def line_copy(src, dst, what, l, delta):
        return pltpu.make_async_remote_copy(
            src, dst, line_send.at[what, l], line_recv.at[what, l],
            device_id=(peer(delta), lev), device_id_type=MESH,
        )

    rest = pl.ds(1, RING - 1)
    others = pl.ds(1, 2 * RING - 1)

    def line_all(what, l):
        ref = seed_in.at[l, rest] if what == 0 else (ask_in if what == 1 else answer_in).at[l, others]
        return line_copy(ref, ref, what, l, (0, 0, 1))

    for e in OUTWARD:
        for l in range(2):
            line_copy(seed_out.at[l], seed_in.at[l, RING - e], 0, l, along(l, e)).start()
    for q in ACROSS:
        for l in range(2):
            line_copy(ask_out.at[l, q], ask_in.at[l, q], 1, l, across(l, q)).start()

    def halo_copy(src, dst, s, device):
        return pltpu.make_async_remote_copy(
            src, dst, halo_send.at[s], halo_recv.at[s], device_id=device, device_id_type=MESH
        )

    def start_halo(k):
        x = x_buf.at[k]
        into = halo_x.at[k]
        halo_copy(x, into.at[pl.ds(0, 4)], k, (me, above)).start()
        halo_copy(x, into.at[pl.ds(4, 4)], k, (me, below)).start()
        halo_copy(x, into.at[pl.ds(8, 4)], k, (north, lev)).start()
        halo_copy(x, into.at[pl.ds(12, 4)], k, (south, lev)).start()
        halo_copy(x.at[3], into.at[16], k, (north, above)).start()
        halo_copy(x.at[2], into.at[17], k, (south, above)).start()
        halo_copy(x.at[1], into.at[18], k, (north, below)).start()
        halo_copy(x.at[0], into.at[19], k, (south, below)).start()

    def halo_all(k):
        return halo_copy(halo_x.at[k], halo_x.at[k], k, (north, lev))

    def start_kappa():
        halo_copy(k_buf.at[pl.ds(2, 2)], halo_k.at[pl.ds(0, 2)], STEPS, (me, above)).start()
        halo_copy(k_buf.at[pl.ds(0, 2)], halo_k.at[pl.ds(2, 2)], STEPS, (me, below)).start()
        for l in range(2):
            halo_copy(k_buf.at[2 * l + 1], halo_k.at[4 + l], STEPS, (north, lev)).start()
            halo_copy(k_buf.at[2 * l], halo_k.at[6 + l], STEPS, (south, lev)).start()

    def kappa_all():
        return halo_copy(halo_k, halo_k, STEPS, (north, lev))

    start_halo(0)
    start_kappa()

    slot_peer = slot_ref[0:1, :]
    slot_y, slot_z, slot_c = slot_ref[1:2, :], slot_ref[2:3, :], slot_ref[3:4, :]
    slot_peer = ((y + slot_y) % RING) * (2 * RING) + ((z + slot_z) % RING) * 2 + (c + slot_c) % 2
    slot_j = iota((1, ROWS), 1) % SLOTS
    block_j = 2 * level_of + rank
    pick = ((owner == slot_peer) & (block_j == slot_j)).astype(F32)
    pick_ref[...] = pick.astype(BF)
    pick_t = pick.T.astype(BF)
    pick_t_ref[...] = pick_t
    cells = jnp.concatenate([cell_ref[0:1, :], cell_ref[1:2, :]], axis=1)
    cell_t = ((row_i // 64 == col_i // 64) & (row_i % 64 == cells)).astype(BF)
    cell = cell_t.T

    for load in loads[5:]:
        load.wait()
    block_row = iota((1, 128), 1)
    lives = jnp.where(block_row < 64, live_ref[0:1, 0:1], live_ref[0:1, 1:2])
    alive = (block_row % 64 < lives).astype(F32)
    spread = (iota((16, 256), 1) % 16 == iota((16, 256), 0)).astype(F32)
    own = (iota((128, 256), 1) // 16 == iota((128, 256), 0) % 16).astype(F32)
    gain = jnp.concatenate([prec_ref[0], prec_ref[1]], axis=1) * alive
    offset = gain * jnp.concatenate([value_ref[0], value_ref[1]], axis=1)
    gain_ref[...] = dot(gain.T, spread, precision=lax.Precision.HIGHEST) * own
    offset_ref[...] = dot(offset.T, spread, precision=lax.Precision.HIGHEST) * own
    for p in range(8):
        w = weight_ref[p // 4, 16 * (p % 4) : 16 * (p % 4) + 16].reshape(256, 128)
        weight_t_ref[p] = w.T

    def trip_copy(t, i, delta):
        if t in (2, 4):
            delta = negative(delta)
        part = int(i >= FAR)
        return pltpu.make_async_remote_copy(
            trip_out.at[t, i], trip_in.at[t, i], trip_send.at[t, part], trip_recv.at[t, part],
            device_id=(peer(delta), lev), device_id_type=MESH,
        )

    def trip_part(t, part):
        span = pl.ds(0, FAR) if part == 0 else pl.ds(FAR, SELF - FAR)
        return pltpu.make_async_remote_copy(
            trip_out.at[t, span], trip_in.at[t, span], trip_send.at[t, part], trip_recv.at[t, part],
            device_id=(north, lev), device_id_type=MESH,
        )

    def start_trip(t, lhs, rhs):
        for part, (lo, hi) in enumerate(((0, FAR), (FAR, GROUPS))):
            rows = lhs[SLOTS * lo : SLOTS * hi]
            groups = dot(rows, rhs).astype(BF).reshape(hi - lo, SLOTS, 128)
            trip_out[t, lo:hi] = groups
            for i in range(lo, min(hi, SELF)):
                trip_copy(t, i, PEERS[i]).start()
            if part == 1:
                trip_in[t, SELF] = groups[SELF - lo]

    def finish_trip(t, lhs):
        trip_part(t, 1).wait_recv()
        total = dot(lhs[:, SLOTS * FAR :], trip_in[t, FAR:].reshape(ROWS - SLOTS * FAR, 128))
        trip_part(t, 0).wait_recv()
        return total + dot(lhs[:, : SLOTS * FAR], trip_in[t, :FAR].reshape(SLOTS * FAR, 128))

    lane = iota((32, 128), 1)
    has = {
        (-1, 0): lev > 0, (1, 0): lev < 3, (0, -1): me > 0, (0, 1): me < tiles - 1,
    }

    def stencil(v, kap, near):
        left = pltpu.roll(v, 1, 1)
        left = jnp.where(lane == 0, pltpu.roll(left, 1, 0), left)
        right = pltpu.roll(v, 127, 1)
        right = jnp.where(lane == 127, pltpu.roll(right, 31, 0), right)
        return (kap + 6.0) * v - (near + left + right)

    def prior(k):
        halo_all(k).wait_recv()
        if k == 0:
            kappa_all().wait_recv()
        v, kap = {}, {}
        for l in range(2):
            for r in range(2):
                v[l, r] = x_buf[k, 2 * l + r]
                kap[l, r] = k_buf[2 * l + r]
                v[l - 2, r] = halo_x[k, 2 * l + r]
                v[l + 2, r] = halo_x[k, 4 + 2 * l + r]
                v[l, r - 2] = halo_x[k, 8 + 2 * l + r]
                v[l, r + 2] = halo_x[k, 12 + 2 * l + r]
        v[-1, -1], v[-1, 2], v[2, -1], v[2, 2] = (halo_x[k, 16 + q] for q in range(4))
        for q in range(2):
            kap[-1, q], kap[2, q] = halo_k[q], halo_k[2 + q]
            kap[q, -1], kap[q, 2] = halo_k[4 + q], halo_k[6 + q]

        def inside(l, r):
            conds = []
            if l < 0:
                conds.append(has[-1, 0])
            if l > 1:
                conds.append(has[1, 0])
            if r < 0:
                conds.append(has[0, -1])
            if r > 1:
                conds.append(has[0, 1])
            return conds

        def masked(p, l, r):
            for cond in inside(l, r):
                p = jnp.where(cond, p, 0.0)
            return p

        v = {at: masked(p, *at) for at, p in v.items()}
        once = {}
        for l, r in list(kap):
            near = v[l - 1, r] + v[l + 1, r] + v[l, r - 1] + v[l, r + 1]
            once[l, r] = masked(stencil(v[l, r], kap[l, r], near), l, r)
        planes = []
        for l in range(2):
            for r in range(2):
                near = once[l - 1, r] + once[l + 1, r] + once[l, r - 1] + once[l, r + 1]
                twice = stencil(once[l, r], kap[l, r], near)
                noise = noise_ref[k, l, r : r + 1, :].reshape(32, 128)
                planes.append(v[l, r] - STEP * twice + NOISE_SCALE * noise)
        return planes

    for l in range(2):
        line_all(1, l).wait_recv()
        line_all(0, l).wait_recv()
        asked = ask_in[l].reshape(256, 128)
        row_e, lane_e = (iota((256, 128), 0) // 2) % RING, iota((256, 128), 1) // 64
        wide = jnp.concatenate(
            [jnp.where(row_e == 2 * m + lane_e, asked, jnp.zeros_like(asked)) for m in range(RING // 2)], axis=1
        )
        answer = dot(wide, seed_in[l].reshape(512, 128)).astype(BF).reshape(2 * RING, LINE_ROWS, 128)
        answer_out[l] = answer
        answer_in[l, 0] = answer[0]
        for q in ACROSS:
            line_copy(answer_out.at[l, q], answer_in.at[l, q], 2, l, negative(across(l, q))).start()
    start_trip(0, pick_t, cell)

    for k in range(STEPS):
        if k > 0:
            start_trip(2 * k, trip_in[0].reshape(ROWS, 128), x_buf[k].reshape(128, 128).astype(BF))
            start_halo(k)
        planes = prior(k)
        if k > 0:
            cells_in = finish_trip(2 * k, pick_ref).astype(BF)
        else:
            halves = []
            for l in range(2):
                line_all(2, l).wait_recv()
                halves.append(dot(pick_line_ref[l], answer_in[l].reshape(256, 128)))
            cells_in = jnp.concatenate(halves, axis=0).astype(BF)
        parts = []
        for p in range(8):
            seen = dot(cells_in[16 * p : 16 * p + 16], weight_t_ref[p])
            misfit = gain_ref[16 * p : 16 * p + 16] * seen - offset_ref[16 * p : 16 * p + 16]
            w = weight_ref[p // 4, 16 * (p % 4) : 16 * (p % 4) + 16].reshape(256, 128)
            parts.append(dot(misfit.astype(BF), w).astype(BF))
        start_trip(1 + 2 * k, pick_t_ref, jnp.concatenate(parts, axis=0))
        if k == 0:
            trip_part(0, 0).wait_recv()
            trip_part(0, 1).wait_recv()
            wanted_t_ref[...] = trip_in[0].reshape(ROWS, 128).T
        total = finish_trip(1 + 2 * k, wanted_t_ref)
        for l in range(2):
            for r in range(2):
                q = 2 * l + r
                new = planes[q] - STEP * total[32 * q : 32 * q + 32]
                if k + 1 < STEPS:
                    x_buf[k + 1, q] = new
                else:
                    out_ref[l, r : r + 1, :] = new.reshape(1, 4096)

    for what in range(3):
        for l in range(2):
            line_all(what, l).wait_send()
    for t in range(2 * STEPS):
        trip_part(t, 0).wait_send()
        trip_part(t, 1).wait_send()
    for k in range(STEPS):
        halo_all(k).wait_send()
    kappa_all().wait_send()


def per_device(
    slots, field, kappa_sq, noise, block_owner, block_cell, live_count, obs_weight, obs_value, obs_prec
):
    operands = (
        slots, field, kappa_sq, noise, block_owner.transpose(0, 2, 1), block_cell, live_count.transpose(1, 0),
        obs_weight, obs_value.transpose(0, 2, 1), obs_prec.transpose(0, 2, 1),
    )
    trips = 2 * STEPS
    return pl.pallas_call(
        kernel_body,
        out_shape=jax.ShapeDtypeStruct((2, 2, 4096), F32),
        in_specs=[pl.BlockSpec(memory_space=pltpu.HBM)] * 10,
        out_specs=pl.BlockSpec(memory_space=pltpu.VMEM),
        scratch_shapes=[
            *[pltpu.VMEM(a.shape, a.dtype) for a in operands],
            pltpu.VMEM((trips, GROUPS, SLOTS, 128), BF),
            pltpu.VMEM((trips, GROUPS, SLOTS, 128), BF),
            pltpu.VMEM((STEPS, 20, 32, 128), F32),
            pltpu.VMEM((8, 32, 128), F32),
            pltpu.VMEM((STEPS, 4, 32, 128), F32),
            pltpu.VMEM((4, 32, 128), F32),
            pltpu.VMEM((128, ROWS), BF),
            pltpu.VMEM((ROWS, 128), BF),
            pltpu.VMEM((128, 256), F32),
            pltpu.VMEM((128, 256), F32),
            pltpu.VMEM((8, 128, 256), BF),
            pltpu.VMEM((128, ROWS), BF),
            pltpu.VMEM((2, 64, 128), BF),
            pltpu.VMEM((2, RING, 64, 128), BF),
            *[pltpu.VMEM((2, 2 * RING, LINE_ROWS, 128), BF)] * 4,
            pltpu.VMEM((2, 64, 256), BF),
            pltpu.SemaphoreType.DMA((trips, 2)),
            pltpu.SemaphoreType.DMA((trips, 2)),
            pltpu.SemaphoreType.DMA((STEPS + 1,)),
            pltpu.SemaphoreType.DMA((STEPS + 1,)),
            pltpu.SemaphoreType.DMA((10,)),
            pltpu.SemaphoreType.DMA((3, 2)),
            pltpu.SemaphoreType.DMA((3, 2)),
        ],
        compiler_params=pltpu.CompilerParams(
            collective_id=0, has_side_effects=True, vmem_limit_bytes=60 << 20
        ),
        cost_estimate=pl.CostEstimate(flops=200_000_000, bytes_accessed=1_000_000, transcendentals=0),
    )(*operands)


def slot_table():
    deltas = PEERS + [(0, 0, 0)]
    table = [[0] * ROWS for _ in range(8)]
    for i, delta in enumerate(deltas):
        for j in range(SLOTS):
            for q in range(3):
                table[1 + q][SLOTS * i + j] = delta[q]
    return jnp.array(table, jnp.int32)


def solution(mesh):
    placed = (
        P("lev", "tile", None),
        P("lev", "tile", None),
        P(None, "lev", "tile", None),
        P("lev", "tile", None),
        P("lev", "tile"),
        P("lev", "tile"),
        P("lev", "tile", None, None),
        P("lev", "tile", None),
        P("lev", "tile", None),
    )
    run = jax.shard_map(
        per_device, mesh=mesh, in_specs=(P(None, None),) + placed, out_specs=P("lev", "tile", None), check_vma=False
    )

    def sample(*arrays):
        return run(slot_table(), *arrays)

    return sample
```

```python
import functools

import jax
import jax.numpy as jnp
from jax import lax
from jax.sharding import PartitionSpec as P
from jax.experimental import pallas as pl
from jax.experimental.pallas import tpu as pltpu

STEPS = 3
STEP = 0.003
NOISE_SCALE = (2.0 * STEP) ** 0.5
MESH = pl.DeviceIdType.MESH
BF = jnp.bfloat16
F32 = jnp.float32
RING = 8


def ring_distance(d):
    return min(d, RING - d)


def hops(delta):
    return ring_distance(delta[0]) + ring_distance(delta[1])


PEERS = sorted(
    [(a, b, c) for a in range(RING) for b in range(RING) for c in range(2) if (a, b, c) != (0, 0, 0)],
    key=lambda d: (-hops(d), (d[0] + 3 * d[1]) % 4, d),
)
SELF = len(PEERS)
GROUPS = SELF + 1
SLOTS = 4
ROWS = GROUPS * SLOTS
FAR = 32

OUTWARD = (4, 3, 5, 2, 6, 1, 7)
LINE_ROWS = 2 * RING


def along(l, e):
    return (e, 0, 0) if l == 0 else (0, e, 0)


def across(l, q):
    return (0, q // 2, q % 2) if l == 0 else (q // 2, 0, q % 2)


def negative(delta):
    return ((RING - delta[0]) % RING, (RING - delta[1]) % RING, delta[2])


ACROSS = [2 * d + c for d in OUTWARD for c in (1, 0)] + [1]
GREETED = sorted({across(l, q) for l in range(2) for q in ACROSS})


def dot(a, b, dims=((1,), (0,)), **kw):
    return lax.dot_general(a, b, (dims, ((), ())), preferred_element_type=F32, **kw)


def iota(shape, dim):
    return lax.broadcasted_iota(jnp.int32, shape, dim)


def kernel_body(
    slot_hbm, field_hbm, kappa_hbm, noise_hbm, owner_hbm, cell_hbm, live_hbm, weight_hbm, value_hbm, prec_hbm,
    out_ref,
    slot_ref, field_ref, kappa_ref, noise_ref, owner_ref, cell_ref, live_ref, weight_ref, value_ref, prec_ref,
    trip_out, trip_in, near_x, far_x, halo_k, x_buf, k_buf, x_sent, k_sent, pick_ref, pick_t_ref, gain_ref, offset_ref, weight_t_ref,
    wanted_t_ref, seed_out, seed_in, ask_out, ask_in, answer_out, answer_in, pick_line_ref,
    trip_send, trip_recv, halo_send, halo_recv, load_sem, line_send, line_recv,
):
    me = lax.axis_index("tile")
    lev = lax.axis_index("lev")
    tiles = 2 * RING * RING
    y, z, c = me // (2 * RING), (me // 2) % RING, me % 2
    at_y = [((y + d) % RING) * (2 * RING) for d in range(RING)]
    at_z = [((z + d) % RING) * 2 for d in range(RING)]
    at_c = [c, 1 - c]

    def peer(delta):
        return at_y[delta[0]] + at_z[delta[1]] + at_c[delta[2]]

    above, below = (lev + 1) % 4, (lev + 3) % 4
    north, south = (me + 1) % tiles, (me + tiles - 1) % tiles

    greet = pltpu.get_barrier_semaphore()
    for delta in GREETED:
        pl.semaphore_signal(greet, inc=1, device_id=(peer(delta), lev), device_id_type=MESH)
    beside = [(north, lev), (south, lev), (me, above), (me, below), (north, above), (north, below), (south, above), (south, below)]
    for device in beside:
        pl.semaphore_signal(greet, inc=1, device_id=device, device_id_type=MESH)

    loads = [
        pltpu.make_async_copy(src, dst, load_sem.at[i])
        for i, (src, dst) in enumerate(
            [
                (owner_hbm, owner_ref), (cell_hbm, cell_ref), (slot_hbm, slot_ref), (field_hbm, field_ref),
                (kappa_hbm, kappa_ref), (live_hbm, live_ref), (prec_hbm, prec_ref), (value_hbm, value_ref),
                (weight_hbm, weight_ref), (noise_hbm, noise_ref),
            ]
        )
    ]
    for load in loads:
        load.start()
    for load in loads[:5]:
        load.wait()
    for l in range(2):
        for r in range(2):
            x_plane = field_ref[l, r : r + 1, :].reshape(32, 128)
            k_plane = kappa_ref[l, r : r + 1, :].reshape(32, 128)
            x_buf[0, 2 * l + r], x_sent[0, 2 * l + r] = x_plane, x_plane.astype(BF)
            k_buf[2 * l + r], k_sent[2 * l + r] = k_plane, k_plane.astype(BF)

    owner_row = jnp.concatenate([owner_ref[0], owner_ref[1]], axis=1).astype(F32)
    owner = jnp.broadcast_to(owner_row, (128, 128)).T.astype(jnp.int32)[:, 0:1]
    level_of = iota((128, 1), 0) // 64
    row_i, col_i = iota((128, 128), 0), iota((128, 128), 1)
    named = (owner == col_i).astype(F32)
    before = ((col_i < row_i) & (col_i // 64 == row_i // 64)).astype(BF)
    rank = jnp.sum(dot(before, named.astype(BF)) * named, axis=1, keepdims=True).astype(jnp.int32)
    n = iota((1, 256), 1)
    for l in range(2):
        x_flat = x_sent[0, 2 * l : 2 * l + 2].reshape(64, 128)
        seed_out[l] = x_flat
        seed_in[l, 0] = x_flat
        e, d = (n // 2) % RING, n // 32
        dy, dz = (e, d) if l == 0 else (d, e)
        line_peer = ((y + dy) % RING) * (2 * RING) + ((z + dz) % RING) * 2 + (c + (n // 16) % 2) % 2
        mine = slice(64 * l, 64 * l + 64)
        pick_line = ((owner[mine] == line_peer) & (rank[mine] == n % 2)).astype(F32)
        pick_line_ref[l] = pick_line.astype(BF)
        cell_line = (row_i[:, :64] % 64 == cell_ref[l : l + 1, :]).astype(F32).T.astype(BF)
        ask = dot(pick_line.T.astype(BF), cell_line).astype(BF).reshape(2 * RING, LINE_ROWS, 128)
        ask_out[l] = ask
        ask_in[l, 0] = ask[0]

    pl.semaphore_wait(greet, len(GREETED) + len(beside))

    def line_copy(src, dst, what, l, delta):
        return pltpu.make_async_remote_copy(
            src, dst, line_send.at[what, l], line_recv.at[what, l],
            device_id=(peer(delta), lev), device_id_type=MESH,
        )

    rest = pl.ds(1, RING - 1)
    others = pl.ds(1, 2 * RING - 1)

    def line_all(what, l):
        ref = seed_in.at[l, rest] if what == 0 else (ask_in if what == 1 else answer_in).at[l, others]
        return line_copy(ref, ref, what, l, (0, 0, 1))

    for q in ACROSS:
        for l in range(2):
            line_copy(ask_out.at[l, q], ask_in.at[l, q], 1, l, across(l, q)).start()
    for e in OUTWARD:
        for l in range(2):
            line_copy(seed_out.at[l], seed_in.at[l, RING - e], 0, l, along(l, e)).start()

    def halo_copy(src, dst, kind, s, device):
        return pltpu.make_async_remote_copy(
            src, dst, halo_send.at[kind, s], halo_recv.at[kind, s], device_id=device, device_id_type=MESH
        )

    def start_halo(k):
        x, sent = x_buf.at[k], x_sent.at[k]
        near, far = near_x.at[k], far_x.at[k]
        halo_copy(x.at[pl.ds(2, 2)], near.at[pl.ds(0, 2)], 0, k, (me, above)).start()
        halo_copy(x.at[pl.ds(0, 2)], near.at[pl.ds(2, 2)], 0, k, (me, below)).start()
        halo_copy(sent.at[pl.ds(0, 2)], far.at[pl.ds(0, 2)], 1, k, (me, above)).start()
        halo_copy(sent.at[pl.ds(2, 2)], far.at[pl.ds(2, 2)], 1, k, (me, below)).start()
        for l in range(2):
            halo_copy(x.at[2 * l + 1], near.at[4 + l], 0, k, (north, lev)).start()
            halo_copy(x.at[2 * l], near.at[6 + l], 0, k, (south, lev)).start()
            halo_copy(sent.at[2 * l], far.at[4 + l], 1, k, (north, lev)).start()
            halo_copy(sent.at[2 * l + 1], far.at[6 + l], 1, k, (south, lev)).start()
        halo_copy(sent.at[3], far.at[8], 1, k, (north, above)).start()
        halo_copy(sent.at[2], far.at[9], 1, k, (south, above)).start()
        halo_copy(sent.at[1], far.at[10], 1, k, (north, below)).start()
        halo_copy(sent.at[0], far.at[11], 1, k, (south, below)).start()

    def halo_all(k):
        return [
            halo_copy(ref.at[k], ref.at[k], kind, k, (north, lev)) for kind, ref in enumerate((near_x, far_x))
        ]

    def start_kappa():
        halo_copy(k_sent.at[pl.ds(2, 2)], halo_k.at[pl.ds(0, 2)], 1, STEPS, (me, above)).start()
        halo_copy(k_sent.at[pl.ds(0, 2)], halo_k.at[pl.ds(2, 2)], 1, STEPS, (me, below)).start()
        for l in range(2):
            halo_copy(k_sent.at[2 * l + 1], halo_k.at[4 + l], 1, STEPS, (north, lev)).start()
            halo_copy(k_sent.at[2 * l], halo_k.at[6 + l], 1, STEPS, (south, lev)).start()

    def kappa_all():
        return halo_copy(halo_k, halo_k, 1, STEPS, (north, lev))

    slot_peer = slot_ref[0:1, :]
    slot_y, slot_z, slot_c = slot_ref[1:2, :], slot_ref[2:3, :], slot_ref[3:4, :]
    slot_peer = ((y + slot_y) % RING) * (2 * RING) + ((z + slot_z) % RING) * 2 + (c + slot_c) % 2
    slot_j = iota((1, ROWS), 1) % SLOTS
    block_j = 2 * level_of + rank
    pick = ((owner == slot_peer) & (block_j == slot_j)).astype(F32)
    pick_ref[...] = pick.astype(BF)
    pick_t = pick.T.astype(BF)
    pick_t_ref[...] = pick_t
    cells = jnp.concatenate([cell_ref[0:1, :], cell_ref[1:2, :]], axis=1)
    cell_t = ((row_i // 64 == col_i // 64) & (row_i % 64 == cells)).astype(BF)
    cell = cell_t.T

    for load in loads[5:]:
        load.wait()
    block_row = iota((1, 128), 1)
    lives = jnp.where(block_row < 64, live_ref[0:1, 0:1], live_ref[0:1, 1:2])
    alive = (block_row % 64 < lives).astype(F32)
    spread = (iota((16, 256), 1) % 16 == iota((16, 256), 0)).astype(F32)
    own = (iota((128, 256), 1) // 16 == iota((128, 256), 0) % 16).astype(F32)
    gain = jnp.concatenate([prec_ref[0], prec_ref[1]], axis=1) * alive
    offset = gain * jnp.concatenate([value_ref[0], value_ref[1]], axis=1)
    gain_ref[...] = dot(gain.T, spread, precision=lax.Precision.HIGHEST) * own
    offset_ref[...] = dot(offset.T, spread, precision=lax.Precision.HIGHEST) * own
    for p in range(8):
        w = weight_ref[p // 4, 16 * (p % 4) : 16 * (p % 4) + 16].reshape(256, 128)
        weight_t_ref[p] = w.T

    def trip_copy(t, i, delta):
        if t in (2, 4):
            delta = negative(delta)
        part = int(i >= FAR)
        return pltpu.make_async_remote_copy(
            trip_out.at[t, i], trip_in.at[t, i], trip_send.at[t, part], trip_recv.at[t, part],
            device_id=(peer(delta), lev), device_id_type=MESH,
        )

    def trip_part(t, part):
        span = pl.ds(0, FAR) if part == 0 else pl.ds(FAR, SELF - FAR)
        return pltpu.make_async_remote_copy(
            trip_out.at[t, span], trip_in.at[t, span], trip_send.at[t, part], trip_recv.at[t, part],
            device_id=(north, lev), device_id_type=MESH,
        )

    def start_trip(t, lhs, rhs):
        for part, (lo, hi) in enumerate(((0, FAR), (FAR, GROUPS))):
            rows = lhs[SLOTS * lo : SLOTS * hi]
            groups = dot(rows, rhs).astype(BF).reshape(hi - lo, SLOTS, 128)
            trip_out[t, lo:hi] = groups
            for i in range(lo, min(hi, SELF)):
                trip_copy(t, i, PEERS[i]).start()
            if part == 1:
                trip_in[t, SELF] = groups[SELF - lo]

    def finish_trip(t, lhs, meanwhile=None):
        trip_part(t, 1).wait_recv()
        if meanwhile is not None:
            meanwhile()
        total = dot(lhs[:, SLOTS * FAR :], trip_in[t, FAR:].reshape(ROWS - SLOTS * FAR, 128))
        trip_part(t, 0).wait_recv()
        return total + dot(lhs[:, : SLOTS * FAR], trip_in[t, :FAR].reshape(SLOTS * FAR, 128))

    lane = iota((32, 128), 1)
    has = {
        (-1, 0): lev > 0, (1, 0): lev < 3, (0, -1): me > 0, (0, 1): me < tiles - 1,
    }

    def stencil(v, kap, near):
        left = pltpu.roll(v, 1, 1)
        left = jnp.where(lane == 0, pltpu.roll(left, 1, 0), left)
        right = pltpu.roll(v, 127, 1)
        right = jnp.where(lane == 127, pltpu.roll(right, 31, 0), right)
        return (kap + 6.0) * v - (near + left + right)

    def prior(k):
        for copy in halo_all(k):
            copy.wait_recv()
        if k == 0:
            kappa_all().wait_recv()
        v, kap = {}, {}
        for l in range(2):
            for r in range(2):
                v[l, r] = x_buf[k, 2 * l + r]
                kap[l, r] = k_buf[2 * l + r]
        for q in range(2):
            v[-1, q], v[2, q], v[q, -1], v[q, 2] = (near_x[k, 2 * side + q] for side in range(4))
            v[-2, q], v[3, q], v[q, -2], v[q, 3] = (far_x[k, 2 * side + q].astype(F32) for side in range(4))
        v[-1, -1], v[-1, 2], v[2, -1], v[2, 2] = (far_x[k, 8 + q].astype(F32) for q in range(4))
        for q in range(2):
            kap[-1, q], kap[2, q] = halo_k[q].astype(F32), halo_k[2 + q].astype(F32)
            kap[q, -1], kap[q, 2] = halo_k[4 + q].astype(F32), halo_k[6 + q].astype(F32)

        def inside(l, r):
            conds = []
            if l < 0:
                conds.append(has[-1, 0])
            if l > 1:
                conds.append(has[1, 0])
            if r < 0:
                conds.append(has[0, -1])
            if r > 1:
                conds.append(has[0, 1])
            return conds

        def masked(p, l, r):
            for cond in inside(l, r):
                p = jnp.where(cond, p, 0.0)
            return p

        v = {at: masked(p, *at) for at, p in v.items()}
        once = {}
        for l, r in list(kap):
            near = v[l - 1, r] + v[l + 1, r] + v[l, r - 1] + v[l, r + 1]
            once[l, r] = masked(stencil(v[l, r], kap[l, r], near), l, r)
        planes = []
        for l in range(2):
            for r in range(2):
                near = once[l - 1, r] + once[l + 1, r] + once[l, r - 1] + once[l, r + 1]
                twice = stencil(once[l, r], kap[l, r], near)
                noise = noise_ref[k, l, r : r + 1, :].reshape(32, 128)
                planes.append(v[l, r] - STEP * twice + NOISE_SCALE * noise)
        return planes

    for l in range(2):
        line_all(1, l).wait_recv()
        line_all(0, l).wait_recv()
        asked = ask_in[l].reshape(256, 128)
        row_e, lane_e = (iota((256, 128), 0) // 2) % RING, iota((256, 128), 1) // 64
        wide = jnp.concatenate(
            [jnp.where(row_e == 2 * m + lane_e, asked, jnp.zeros_like(asked)) for m in range(RING // 2)], axis=1
        )
        answer = dot(wide, seed_in[l].reshape(512, 128)).astype(BF).reshape(2 * RING, LINE_ROWS, 128)
        answer_out[l] = answer
        answer_in[l, 0] = answer[0]
        for q in ACROSS:
            line_copy(answer_out.at[l, q], answer_in.at[l, q], 2, l, negative(across(l, q))).start()

    for k in range(STEPS):
        if k > 0:
            start_trip(2 * k, trip_in[0].reshape(ROWS, 128), x_sent[k].reshape(128, 128))
        else:
            start_trip(0, pick_t, cell)
        if k > 0:
            cells_in = finish_trip(2 * k, pick_ref, functools.partial(start_halo, k)).astype(BF)
        else:
            halves = []
            for l in range(2):
                line_all(2, l).wait_recv()
                if l == 0:
                    start_halo(0)
                    start_kappa()
                halves.append(dot(pick_line_ref[l], answer_in[l].reshape(256, 128)))
            cells_in = jnp.concatenate(halves, axis=0).astype(BF)
        misfits = []
        for p in range(8):
            seen = dot(cells_in[16 * p : 16 * p + 16], weight_t_ref[p])
            misfit = gain_ref[16 * p : 16 * p + 16] * seen - offset_ref[16 * p : 16 * p + 16]
            misfits.append(misfit.astype(BF))
        parts = []
        for p in range(8):
            w = weight_ref[p // 4, 16 * (p % 4) : 16 * (p % 4) + 16].reshape(256, 128)
            parts.append(dot(misfits[p], w).astype(BF))
        start_trip(1 + 2 * k, pick_t_ref, jnp.concatenate(parts, axis=0))
        planes = prior(k)
        if k == 0:
            trip_part(0, 0).wait_recv()
            trip_part(0, 1).wait_recv()
            wanted_t_ref[...] = trip_in[0].reshape(ROWS, 128).T
        total = finish_trip(1 + 2 * k, wanted_t_ref)
        for l in range(2):
            for r in range(2):
                q = 2 * l + r
                new = planes[q] - STEP * total[32 * q : 32 * q + 32]
                if k + 1 < STEPS:
                    x_buf[k + 1, q], x_sent[k + 1, q] = new, new.astype(BF)
                else:
                    out_ref[l, r : r + 1, :] = new.reshape(1, 4096)

    for what in range(3):
        for l in range(2):
            line_all(what, l).wait_send()
    for t in range(2 * STEPS):
        trip_part(t, 0).wait_send()
        trip_part(t, 1).wait_send()
    for k in range(STEPS):
        for copy in halo_all(k):
            copy.wait_send()
    kappa_all().wait_send()


def per_device(
    slots, field, kappa_sq, noise, block_owner, block_cell, live_count, obs_weight, obs_value, obs_prec
):
    operands = (
        slots, field, kappa_sq, noise, block_owner.transpose(0, 2, 1), block_cell, live_count.transpose(1, 0),
        obs_weight, obs_value.transpose(0, 2, 1), obs_prec.transpose(0, 2, 1),
    )
    trips = 2 * STEPS
    return pl.pallas_call(
        kernel_body,
        out_shape=jax.ShapeDtypeStruct((2, 2, 4096), F32),
        in_specs=[pl.BlockSpec(memory_space=pltpu.HBM)] * 10,
        out_specs=pl.BlockSpec(memory_space=pltpu.VMEM),
        scratch_shapes=[
            *[pltpu.VMEM(a.shape, a.dtype) for a in operands],
            pltpu.VMEM((trips, GROUPS, SLOTS, 128), BF),
            pltpu.VMEM((trips, GROUPS, SLOTS, 128), BF),
            pltpu.VMEM((STEPS, 8, 32, 128), F32),
            pltpu.VMEM((STEPS, 12, 32, 128), BF),
            pltpu.VMEM((8, 32, 128), BF),
            pltpu.VMEM((STEPS, 4, 32, 128), F32),
            pltpu.VMEM((4, 32, 128), F32),
            pltpu.VMEM((STEPS, 4, 32, 128), BF),
            pltpu.VMEM((4, 32, 128), BF),
            pltpu.VMEM((128, ROWS), BF),
            pltpu.VMEM((ROWS, 128), BF),
            pltpu.VMEM((128, 256), F32),
            pltpu.VMEM((128, 256), F32),
            pltpu.VMEM((8, 128, 256), BF),
            pltpu.VMEM((128, ROWS), BF),
            pltpu.VMEM((2, 64, 128), BF),
            pltpu.VMEM((2, RING, 64, 128), BF),
            *[pltpu.VMEM((2, 2 * RING, LINE_ROWS, 128), BF)] * 4,
            pltpu.VMEM((2, 64, 256), BF),
            pltpu.SemaphoreType.DMA((trips, 2)),
            pltpu.SemaphoreType.DMA((trips, 2)),
            pltpu.SemaphoreType.DMA((2, STEPS + 1)),
            pltpu.SemaphoreType.DMA((2, STEPS + 1)),
            pltpu.SemaphoreType.DMA((10,)),
            pltpu.SemaphoreType.DMA((3, 2)),
            pltpu.SemaphoreType.DMA((3, 2)),
        ],
        compiler_params=pltpu.CompilerParams(
            collective_id=0, has_side_effects=True, vmem_limit_bytes=40 << 20
        ),
        cost_estimate=pl.CostEstimate(flops=200_000_000, bytes_accessed=1_000_000, transcendentals=0),
    )(*[pltpu.with_memory_space_constraint(a, pltpu.HBM) for a in operands])


def slot_table():
    deltas = PEERS + [(0, 0, 0)]
    table = [[0] * ROWS for _ in range(8)]
    for i, delta in enumerate(deltas):
        for j in range(SLOTS):
            for q in range(3):
                table[1 + q][SLOTS * i + j] = delta[q]
    return jnp.array(table, jnp.int32)


def solution(mesh):
    placed = (
        P("lev", "tile", None),
        P("lev", "tile", None),
        P(None, "lev", "tile", None),
        P("lev", "tile", None),
        P("lev", "tile"),
        P("lev", "tile"),
        P("lev", "tile", None, None),
        P("lev", "tile", None),
        P("lev", "tile", None),
    )
    run = jax.shard_map(
        per_device, mesh=mesh, in_specs=(P(None, None),) + placed, out_specs=P("lev", "tile", None), check_vma=False
    )

    def sample(*arrays):
        return run(slot_table(), *arrays)

    return sample
```

```python
import functools

import jax
import jax.numpy as jnp
from jax import lax
from jax.sharding import PartitionSpec as P
from jax.experimental import pallas as pl
from jax.experimental.pallas import tpu as pltpu

STEPS = 3
STEP = 0.003
NOISE_SCALE = (2.0 * STEP) ** 0.5
MESH = pl.DeviceIdType.MESH
BF = jnp.bfloat16
F32 = jnp.float32
RING = 8


def ring_distance(d):
    return min(d, RING - d)


def hops(delta):
    return ring_distance(delta[0]) + ring_distance(delta[1])


PEERS = sorted(
    [(a, b, c) for a in range(RING) for b in range(RING) for c in range(2) if (a, b, c) != (0, 0, 0)],
    key=lambda d: (-hops(d), d[2], d[0], d[1]),
)
SELF = len(PEERS)
GROUPS = SELF + 1
SLOTS = 4
ROWS = GROUPS * SLOTS
FAR = 64

OUTWARD = (4, 3, 5, 2, 6, 1, 7)
LINE_ROWS = 2 * RING


def along(l, e):
    return (e, 0, 0) if l == 0 else (0, e, 0)


def across(l, q):
    return (0, q // 2, q % 2) if l == 0 else (q // 2, 0, q % 2)


def negative(delta):
    return ((RING - delta[0]) % RING, (RING - delta[1]) % RING, delta[2])


ACROSS = [2 * d + c for d in OUTWARD for c in (1, 0)] + [1]
GREETED = sorted({across(l, q) for l in range(2) for q in ACROSS})


def dot(a, b, dims=((1,), (0,)), **kw):
    return lax.dot_general(a, b, (dims, ((), ())), preferred_element_type=F32, **kw)


def iota(shape, dim):
    return lax.broadcasted_iota(jnp.int32, shape, dim)


def kernel_body(
    slot_hbm, field_hbm, kappa_hbm, noise_hbm, owner_hbm, cell_hbm, live_hbm, weight_hbm, value_hbm, prec_hbm,
    out_ref,
    slot_ref, field_ref, kappa_ref, noise_ref, owner_ref, cell_ref, live_ref, weight_ref, value_ref, prec_ref,
    trip_out, trip_in, near_x, far_x, halo_k, x_buf, k_buf, x_sent, k_sent, pick_ref, pick_t_ref, gain_ref, offset_ref, weight_t_ref,
    wanted_t_ref, seed_out, seed_in, ask_out, ask_in, answer_out, answer_in, pick_line_ref,
    trip_send, trip_recv, halo_send, halo_recv, load_sem, line_send, line_recv,
):
    me = lax.axis_index("tile")
    lev = lax.axis_index("lev")
    tiles = 2 * RING * RING
    y, z, c = me // (2 * RING), (me // 2) % RING, me % 2
    at_y = [((y + d) % RING) * (2 * RING) for d in range(RING)]
    at_z = [((z + d) % RING) * 2 for d in range(RING)]
    at_c = [c, 1 - c]

    def peer(delta):
        return at_y[delta[0]] + at_z[delta[1]] + at_c[delta[2]]

    above, below = (lev + 1) % 4, (lev + 3) % 4
    north, south = (me + 1) % tiles, (me + tiles - 1) % tiles

    greet = pltpu.get_barrier_semaphore()
    for delta in GREETED:
        pl.semaphore_signal(greet, inc=1, device_id=(peer(delta), lev), device_id_type=MESH)
    beside = [(north, lev), (south, lev), (me, above), (me, below), (north, above), (north, below), (south, above), (south, below)]
    for device in beside:
        pl.semaphore_signal(greet, inc=1, device_id=device, device_id_type=MESH)

    loads = [
        pltpu.make_async_copy(src, dst, load_sem.at[i])
        for i, (src, dst) in enumerate(
            [
                (owner_hbm, owner_ref), (cell_hbm, cell_ref), (slot_hbm, slot_ref), (field_hbm, field_ref),
                (kappa_hbm, kappa_ref), (live_hbm, live_ref), (prec_hbm, prec_ref), (value_hbm, value_ref),
                (weight_hbm, weight_ref), (noise_hbm, noise_ref),
            ]
        )
    ]
    for load in loads:
        load.start()
    for load in loads[:5]:
        load.wait()
    for l in range(2):
        for r in range(2):
            x_plane = field_ref[l, r : r + 1, :].reshape(32, 128)
            k_plane = kappa_ref[l, r : r + 1, :].reshape(32, 128)
            x_buf[0, 2 * l + r], x_sent[0, 2 * l + r] = x_plane, x_plane.astype(BF)
            k_buf[2 * l + r], k_sent[2 * l + r] = k_plane, k_plane.astype(BF)

    owner_row = jnp.concatenate([owner_ref[0], owner_ref[1]], axis=1).astype(F32)
    owner = jnp.broadcast_to(owner_row, (128, 128)).T.astype(jnp.int32)[:, 0:1]
    level_of = iota((128, 1), 0) // 64
    row_i, col_i = iota((128, 128), 0), iota((128, 128), 1)
    named = (owner == col_i).astype(F32)
    before = ((col_i < row_i) & (col_i // 64 == row_i // 64)).astype(BF)
    rank = jnp.sum(dot(before, named.astype(BF)) * named, axis=1, keepdims=True).astype(jnp.int32)
    n = iota((1, 256), 1)
    for l in range(2):
        x_flat = x_sent[0, 2 * l : 2 * l + 2].reshape(64, 128)
        seed_out[l] = x_flat
        seed_in[l, 0] = x_flat
        e, d = (n // 2) % RING, n // 32
        dy, dz = (e, d) if l == 0 else (d, e)
        line_peer = ((y + dy) % RING) * (2 * RING) + ((z + dz) % RING) * 2 + (c + (n // 16) % 2) % 2
        mine = slice(64 * l, 64 * l + 64)
        pick_line = ((owner[mine] == line_peer) & (rank[mine] == n % 2)).astype(F32)
        pick_line_ref[l] = pick_line.astype(BF)
        cell_line = (row_i[:, :64] % 64 == cell_ref[l : l + 1, :]).astype(F32).T.astype(BF)
        ask = dot(pick_line.T.astype(BF), cell_line).astype(BF).reshape(2 * RING, LINE_ROWS, 128)
        ask_out[l] = ask
        ask_in[l, 0] = ask[0]

    pl.semaphore_wait(greet, len(GREETED) + len(beside))

    def line_copy(src, dst, what, l, delta):
        return pltpu.make_async_remote_copy(
            src, dst, line_send.at[what, l], line_recv.at[what, l],
            device_id=(peer(delta), lev), device_id_type=MESH,
        )

    rest = pl.ds(1, RING - 1)
    others = pl.ds(1, 2 * RING - 1)

    def line_all(what, l):
        ref = seed_in.at[l, rest] if what == 0 else (ask_in if what == 1 else answer_in).at[l, others]
        return line_copy(ref, ref, what, l, (0, 0, 1))

    for q in ACROSS:
        for l in range(2):
            line_copy(ask_out.at[l, q], ask_in.at[l, q], 1, l, across(l, q)).start()
    for e in OUTWARD:
        for l in range(2):
            line_copy(seed_out.at[l], seed_in.at[l, RING - e], 0, l, along(l, e)).start()

    def halo_copy(src, dst, kind, s, device):
        return pltpu.make_async_remote_copy(
            src, dst, halo_send.at[kind, s], halo_recv.at[kind, s], device_id=device, device_id_type=MESH
        )

    def start_halo(k):
        x, sent = x_buf.at[k], x_sent.at[k]
        near, far = near_x.at[k], far_x.at[k]
        halo_copy(x.at[pl.ds(2, 2)], near.at[pl.ds(0, 2)], 0, k, (me, above)).start()
        halo_copy(x.at[pl.ds(0, 2)], near.at[pl.ds(2, 2)], 0, k, (me, below)).start()
        halo_copy(sent.at[pl.ds(0, 2)], far.at[pl.ds(0, 2)], 1, k, (me, above)).start()
        halo_copy(sent.at[pl.ds(2, 2)], far.at[pl.ds(2, 2)], 1, k, (me, below)).start()
        for l in range(2):
            halo_copy(x.at[2 * l + 1], near.at[4 + l], 0, k, (north, lev)).start()
            halo_copy(x.at[2 * l], near.at[6 + l], 0, k, (south, lev)).start()
            halo_copy(sent.at[2 * l], far.at[4 + l], 1, k, (north, lev)).start()
            halo_copy(sent.at[2 * l + 1], far.at[6 + l], 1, k, (south, lev)).start()
        halo_copy(sent.at[3], far.at[8], 1, k, (north, above)).start()
        halo_copy(sent.at[2], far.at[9], 1, k, (south, above)).start()
        halo_copy(sent.at[1], far.at[10], 1, k, (north, below)).start()
        halo_copy(sent.at[0], far.at[11], 1, k, (south, below)).start()

    def halo_all(k):
        return [
            halo_copy(ref.at[k], ref.at[k], kind, k, (north, lev)) for kind, ref in enumerate((near_x, far_x))
        ]

    def start_kappa():
        halo_copy(k_sent.at[pl.ds(2, 2)], halo_k.at[pl.ds(0, 2)], 1, STEPS, (me, above)).start()
        halo_copy(k_sent.at[pl.ds(0, 2)], halo_k.at[pl.ds(2, 2)], 1, STEPS, (me, below)).start()
        for l in range(2):
            halo_copy(k_sent.at[2 * l + 1], halo_k.at[4 + l], 1, STEPS, (north, lev)).start()
            halo_copy(k_sent.at[2 * l], halo_k.at[6 + l], 1, STEPS, (south, lev)).start()

    def kappa_all():
        return halo_copy(halo_k, halo_k, 1, STEPS, (north, lev))

    slot_peer = slot_ref[0:1, :]
    slot_y, slot_z, slot_c = slot_ref[1:2, :], slot_ref[2:3, :], slot_ref[3:4, :]
    slot_peer = ((y + slot_y) % RING) * (2 * RING) + ((z + slot_z) % RING) * 2 + (c + slot_c) % 2
    slot_j = iota((1, ROWS), 1) % SLOTS
    block_j = 2 * level_of + rank
    pick = ((owner == slot_peer) & (block_j == slot_j)).astype(F32)
    pick_ref[...] = pick.astype(BF)
    pick_t = pick.T.astype(BF)
    pick_t_ref[...] = pick_t
    cells = jnp.concatenate([cell_ref[0:1, :], cell_ref[1:2, :]], axis=1)
    cell_t = ((row_i // 64 == col_i // 64) & (row_i % 64 == cells)).astype(BF)
    cell = cell_t.T

    for load in loads[5:]:
        load.wait()
    block_row = iota((1, 128), 1)
    lives = jnp.where(block_row < 64, live_ref[0:1, 0:1], live_ref[0:1, 1:2])
    alive = (block_row % 64 < lives).astype(F32)
    spread = (iota((16, 256), 1) % 16 == iota((16, 256), 0)).astype(F32)
    own = (iota((128, 256), 1) // 16 == iota((128, 256), 0) % 16).astype(F32)
    gain = jnp.concatenate([prec_ref[0], prec_ref[1]], axis=1) * alive
    offset = gain * jnp.concatenate([value_ref[0], value_ref[1]], axis=1)
    gain_ref[...] = dot(gain.T, spread, precision=lax.Precision.HIGHEST) * own
    offset_ref[...] = dot(offset.T, spread, precision=lax.Precision.HIGHEST) * own
    for p in range(8):
        w = weight_ref[p // 4, 16 * (p % 4) : 16 * (p % 4) + 16].reshape(256, 128)
        weight_t_ref[p] = w.T

    def trip_copy(t, i, delta):
        if t in (2, 4):
            delta = negative(delta)
        part = int(i >= FAR)
        return pltpu.make_async_remote_copy(
            trip_out.at[t, i], trip_in.at[t, i], trip_send.at[t, part], trip_recv.at[t, part],
            device_id=(peer(delta), lev), device_id_type=MESH,
        )

    def trip_part(t, part):
        span = pl.ds(0, FAR) if part == 0 else pl.ds(FAR, SELF - FAR)
        return pltpu.make_async_remote_copy(
            trip_out.at[t, span], trip_in.at[t, span], trip_send.at[t, part], trip_recv.at[t, part],
            device_id=(north, lev), device_id_type=MESH,
        )

    def start_trip(t, lhs, rhs):
        for part, (lo, hi) in enumerate(((0, FAR), (FAR, GROUPS))):
            rows = lhs[SLOTS * lo : SLOTS * hi]
            groups = dot(rows, rhs).astype(BF).reshape(hi - lo, SLOTS, 128)
            trip_out[t, lo:hi] = groups
            for i in range(lo, min(hi, SELF)):
                trip_copy(t, i, PEERS[i]).start()
            if part == 1:
                trip_in[t, SELF] = groups[SELF - lo]

    def finish_trip(t, lhs, meanwhile=None):
        trip_part(t, 1).wait_recv()
        if meanwhile is not None:
            meanwhile()
        total = dot(lhs[:, SLOTS * FAR :], trip_in[t, FAR:].reshape(ROWS - SLOTS * FAR, 128))
        trip_part(t, 0).wait_recv()
        return total + dot(lhs[:, : SLOTS * FAR], trip_in[t, :FAR].reshape(SLOTS * FAR, 128))

    lane = iota((32, 128), 1)
    has = {
        (-1, 0): lev > 0, (1, 0): lev < 3, (0, -1): me > 0, (0, 1): me < tiles - 1,
    }

    def stencil(v, kap, near):
        left = pltpu.roll(v, 1, 1)
        left = jnp.where(lane == 0, pltpu.roll(left, 1, 0), left)
        right = pltpu.roll(v, 127, 1)
        right = jnp.where(lane == 127, pltpu.roll(right, 31, 0), right)
        return (kap + 6.0) * v - (near + left + right)

    def prior(k):
        for copy in halo_all(k):
            copy.wait_recv()
        if k == 0:
            kappa_all().wait_recv()
        v, kap = {}, {}
        for l in range(2):
            for r in range(2):
                v[l, r] = x_buf[k, 2 * l + r]
                kap[l, r] = k_buf[2 * l + r]
        for q in range(2):
            v[-1, q], v[2, q], v[q, -1], v[q, 2] = (near_x[k, 2 * side + q] for side in range(4))
            v[-2, q], v[3, q], v[q, -2], v[q, 3] = (far_x[k, 2 * side + q].astype(F32) for side in range(4))
        v[-1, -1], v[-1, 2], v[2, -1], v[2, 2] = (far_x[k, 8 + q].astype(F32) for q in range(4))
        for q in range(2):
            kap[-1, q], kap[2, q] = halo_k[q].astype(F32), halo_k[2 + q].astype(F32)
            kap[q, -1], kap[q, 2] = halo_k[4 + q].astype(F32), halo_k[6 + q].astype(F32)

        def inside(l, r):
            conds = []
            if l < 0:
                conds.append(has[-1, 0])
            if l > 1:
                conds.append(has[1, 0])
            if r < 0:
                conds.append(has[0, -1])
            if r > 1:
                conds.append(has[0, 1])
            return conds

        def masked(p, l, r):
            for cond in inside(l, r):
                p = jnp.where(cond, p, 0.0)
            return p

        v = {at: masked(p, *at) for at, p in v.items()}
        once = {}
        for l, r in list(kap):
            near = v[l - 1, r] + v[l + 1, r] + v[l, r - 1] + v[l, r + 1]
            once[l, r] = masked(stencil(v[l, r], kap[l, r], near), l, r)
        planes = []
        for l in range(2):
            for r in range(2):
                near = once[l - 1, r] + once[l + 1, r] + once[l, r - 1] + once[l, r + 1]
                twice = stencil(once[l, r], kap[l, r], near)
                noise = noise_ref[k, l, r : r + 1, :].reshape(32, 128)
                planes.append(v[l, r] - STEP * twice + NOISE_SCALE * noise)
        return planes

    wides = []
    for l in range(2):
        line_all(1, l).wait_recv()
        asked = ask_in[l].reshape(256, 128)
        row_e, lane_e = (iota((256, 128), 0) // 2) % RING, iota((256, 128), 1) // 64
        wides.append(jnp.concatenate(
            [jnp.where(row_e == 2 * m + lane_e, asked, jnp.zeros_like(asked)) for m in range(RING // 2)], axis=1
        ))
    for l in range(2):
        line_all(0, l).wait_recv()
        answer = dot(wides[l], seed_in[l].reshape(512, 128)).astype(BF).reshape(2 * RING, LINE_ROWS, 128)
        answer_out[l] = answer
        answer_in[l, 0] = answer[0]
        for q in ACROSS:
            line_copy(answer_out.at[l, q], answer_in.at[l, q], 2, l, negative(across(l, q))).start()

    for k in range(STEPS):
        if k > 0:
            start_trip(2 * k, trip_in[0].reshape(ROWS, 128), x_sent[k].reshape(128, 128))
        else:
            start_trip(0, pick_t, cell)
        if k > 0:
            cells_in = finish_trip(2 * k, pick_ref, functools.partial(start_halo, k)).astype(BF)
        else:
            halves = []
            for l in range(2):
                line_all(2, l).wait_recv()
                if l == 0:
                    start_halo(0)
                    start_kappa()
                halves.append(dot(pick_line_ref[l], answer_in[l].reshape(256, 128)))
            cells_in = jnp.concatenate(halves, axis=0).astype(BF)
        misfits = []
        for p in range(8):
            seen = dot(cells_in[16 * p : 16 * p + 16], weight_t_ref[p])
            misfit = gain_ref[16 * p : 16 * p + 16] * seen - offset_ref[16 * p : 16 * p + 16]
            misfits.append(misfit.astype(BF))
        parts = []
        for p in range(8):
            w = weight_ref[p // 4, 16 * (p % 4) : 16 * (p % 4) + 16].reshape(256, 128)
            parts.append(dot(misfits[p], w).astype(BF))
        start_trip(1 + 2 * k, pick_t_ref, jnp.concatenate(parts, axis=0))
        planes = prior(k)
        if k == 0:
            trip_part(0, 0).wait_recv()
            trip_part(0, 1).wait_recv()
            wanted_t_ref[...] = trip_in[0].reshape(ROWS, 128).T
        total = finish_trip(1 + 2 * k, wanted_t_ref)
        for l in range(2):
            for r in range(2):
                q = 2 * l + r
                new = planes[q] - STEP * total[32 * q : 32 * q + 32]
                if k + 1 < STEPS:
                    x_buf[k + 1, q], x_sent[k + 1, q] = new, new.astype(BF)
                else:
                    out_ref[l, r : r + 1, :] = new.reshape(1, 4096)

    for what in range(3):
        for l in range(2):
            line_all(what, l).wait_send()
    for t in range(2 * STEPS):
        trip_part(t, 0).wait_send()
        trip_part(t, 1).wait_send()
    for k in range(STEPS):
        for copy in halo_all(k):
            copy.wait_send()
    kappa_all().wait_send()


def per_device(
    slots, field, kappa_sq, noise, block_owner, block_cell, live_count, obs_weight, obs_value, obs_prec
):
    operands = (
        slots, field, kappa_sq, noise, block_owner.transpose(0, 2, 1), block_cell, live_count.transpose(1, 0),
        obs_weight, obs_value.transpose(0, 2, 1), obs_prec.transpose(0, 2, 1),
    )
    trips = 2 * STEPS
    return pl.pallas_call(
        kernel_body,
        out_shape=jax.ShapeDtypeStruct((2, 2, 4096), F32),
        in_specs=[pl.BlockSpec(memory_space=pltpu.HBM)] * 10,
        out_specs=pl.BlockSpec(memory_space=pltpu.VMEM),
        scratch_shapes=[
            *[pltpu.VMEM(a.shape, a.dtype) for a in operands],
            pltpu.VMEM((trips, GROUPS, SLOTS, 128), BF),
            pltpu.VMEM((trips, GROUPS, SLOTS, 128), BF),
            pltpu.VMEM((STEPS, 8, 32, 128), F32),
            pltpu.VMEM((STEPS, 12, 32, 128), BF),
            pltpu.VMEM((8, 32, 128), BF),
            pltpu.VMEM((STEPS, 4, 32, 128), F32),
            pltpu.VMEM((4, 32, 128), F32),
            pltpu.VMEM((STEPS, 4, 32, 128), BF),
            pltpu.VMEM((4, 32, 128), BF),
            pltpu.VMEM((128, ROWS), BF),
            pltpu.VMEM((ROWS, 128), BF),
            pltpu.VMEM((128, 256), F32),
            pltpu.VMEM((128, 256), F32),
            pltpu.VMEM((8, 128, 256), BF),
            pltpu.VMEM((128, ROWS), BF),
            pltpu.VMEM((2, 64, 128), BF),
            pltpu.VMEM((2, RING, 64, 128), BF),
            *[pltpu.VMEM((2, 2 * RING, LINE_ROWS, 128), BF)] * 4,
            pltpu.VMEM((2, 64, 256), BF),
            pltpu.SemaphoreType.DMA((trips, 2)),
            pltpu.SemaphoreType.DMA((trips, 2)),
            pltpu.SemaphoreType.DMA((2, STEPS + 1)),
            pltpu.SemaphoreType.DMA((2, STEPS + 1)),
            pltpu.SemaphoreType.DMA((10,)),
            pltpu.SemaphoreType.DMA((3, 2)),
            pltpu.SemaphoreType.DMA((3, 2)),
        ],
        compiler_params=pltpu.CompilerParams(
            collective_id=0, has_side_effects=True, vmem_limit_bytes=40 << 20
        ),
        cost_estimate=pl.CostEstimate(flops=200_000_000, bytes_accessed=1_000_000, transcendentals=0),
    )(*[pltpu.with_memory_space_constraint(a, pltpu.HBM) for a in operands])


def slot_table():
    deltas = PEERS + [(0, 0, 0)]
    table = [[0] * ROWS for _ in range(8)]
    for i, delta in enumerate(deltas):
        for j in range(SLOTS):
            for q in range(3):
                table[1 + q][SLOTS * i + j] = delta[q]
    return jnp.array(table, jnp.int32)


def solution(mesh):
    placed = (
        P("lev", "tile", None),
        P("lev", "tile", None),
        P(None, "lev", "tile", None),
        P("lev", "tile", None),
        P("lev", "tile"),
        P("lev", "tile"),
        P("lev", "tile", None, None),
        P("lev", "tile", None),
        P("lev", "tile", None),
    )
    run = jax.shard_map(
        per_device, mesh=mesh, in_specs=(P(None, None),) + placed, out_specs=P("lev", "tile", None), check_vma=False
    )

    def sample(*arrays):
        return run(slot_table(), *arrays)

    return sample
```
